768 devices in a mesh: section: 3 (over z_lo), dp: 16 (over z_hi, x), expert: 16 (over y, core).
Axes of the slice: x: 4, y: 8, z: 12 (z_hi: 4, z_lo: 3; z = z_hi * 3 + z_lo), core: 2. Of those that a mesh axis runs over, the one named last changes fastest.
Arguments:
- grad_out: bfloat16 [3, 32768, 2048], P('section', ('dp', 'expert')), may hold values from -6 to 6
- routes: int32 [3, 32768, 2], P('section', ('dp', 'expert')), may hold values from 0 to 15, all different within a row; in each aligned block of 128 rows (0 to 127, 128 to 255, ..., all dimensions but the last counted through in order) at most 20 rows name the same one
- gates: float32 [3, 32768, 2], P('section', ('dp', 'expert')), may hold values from 0.2 to 1
- hidden: bfloat16 [3, 16, 16, 320, 1408], P('section', 'dp', 'expert'), may hold values from -0.09375 to 0.09375
- w_down: bfloat16 [3, 16, 1408, 2048], P('section', 'expert'), may hold values from -0.15625 to 0.15625
Outputs:
- grad_hidden: bfloat16 [3, 16, 16, 320, 1408], P('section', 'dp', 'expert')
- grad_w_down: float32 [3, 16, 1408, 2048], P('section', 'expert', 'dp')
The draws below stay inside these ranges and needn't reach their ends.
Inputs may be any that keep to these rules, and one draw needn't show every extreme that they name: `routes`: each token names 2 different experts; among the 128 tokens of one device no expert is named more than 20 times, a bound that some block reaches.
All inputs are finite; a program needn't handle non-finite values.
Results may differ from the reference program's by a relative error of at most 0.015.
Values may be sent and summed in bfloat16 or wider, within the bound.
A program may use at most 64 MiB of HBM per device.

```python
import math
import jax
import jax.numpy as jnp
import numpy as np
from jax import lax

D = 2048
H = 1408
TOPK = 2
TOK_DEV = 128
EXPERTS = 16
CAP = 20
SLOTS = 320
TOKENS = 32768
N_SECTION = 3
N_DP = 16
N_EXPERT = 16


def with_spikes(array, stream_key, source, target, blocks, factor):
    def block_of(dim):
        return (jnp.arange(array.shape[dim]) // (array.shape[dim] // blocks)).reshape((-1,) + (1,) * (array.ndim - 1 - dim))

    near = jax.random.permutation(stream_key, blocks)[block_of(target)]
    second = (block_of(target) + blocks // 2) % blocks
    return jnp.where((block_of(source) == near) | (block_of(source) == second), factor * array, array)


def block_levels(own_key, dims, split, low, top_value):
    factor_of, own = 1.0, jax.random.fold_in(own_key, 6)
    for axis_at, blocks in split:
        steps = jnp.exp(jax.random.uniform(jax.random.fold_in(own, axis_at), (blocks,), jnp.float32, low / len(split), top_value / len(split)))
        factor_of = factor_of * jnp.repeat(steps, dims[axis_at] // blocks).reshape([-1 if axis == axis_at else 1 for axis in range(len(dims))])
    return factor_of


def assign_block(key, own, number, rows, count, top, reach, lean):
    ranking = jax.random.permutation(key, count)
    crowded, common = shares(count, rows * top, reach, lean, True), shares(count, rows * top, reach, lean, False)
    places = jnp.arange(count)

    def named(tallies, turn):
        used = int((tallies > 0).sum())
        fixed = max(1, used // 4)
        moved = fixed + (places - fixed + turn * (used - fixed)) % max(1, count - fixed)
        return jnp.zeros((count,), jnp.int32).at[ranking[jnp.where(places < fixed, places, moved)]].set(jnp.asarray(tallies, jnp.int32))

    tallies = jnp.where(number % 4 == 0, named(crowded, number // 4), named(common, number - number // 4 - 1))
    mixed = jax.random.permutation(jax.random.fold_in(own, 3), count)
    donor, taker = mixed[0:count // 2 * 2:2], mixed[1:count // 2 * 2:2]
    margin = jnp.minimum(tallies[donor] - 1, reach - tallies[taker]) // 2
    margin = jnp.where((donor == ranking[0]) | (taker == ranking[0]) | (tallies[taker] == 0), 0, jnp.maximum(margin, 0))
    moved = jax.random.randint(jax.random.fold_in(own, 4), (count // 2,), 0, 1 << 20) % (margin + 1)
    tallies = tallies.at[donor].add(-moved).at[taker].add(moved)
    members = jnp.searchsorted(jnp.cumsum(tallies), jnp.arange(rows * top), side="right").astype(jnp.int32)
    grid = members.reshape(top, rows).T
    grid = grid[jax.random.permutation(jax.random.fold_in(own, 1), rows)]
    turn = jax.random.randint(jax.random.fold_in(own, 2), (rows, 1), 0, top)
    return jnp.take_along_axis(grid, (jnp.arange(top)[None, :] + turn) % top, axis=1)


def shares(amount, total, bound, skew, full):
    portions = [(1 << 20) // math.isqrt(rank ** skew) + 1 for rank in range(1, amount + 1)]
    largest = bound if full else min(bound, max(-(-total // amount), total * portions[0] // sum(portions)))
    least = 1 if total - largest >= amount - 1 else 0
    given, rest = [largest] + [least] * (amount - 1), total - largest - least * (amount - 1)
    while rest > 0:
        candidates = [i for i in range(1, amount) if given[i] < largest] or [i for i in range(1, amount) if given[i] < bound]
        whole, budget = sum([portions[i] for i in candidates]), rest
        for i in candidates:
            addition = min(bound - given[i], max(1, budget * portions[i] // whole), rest)
            given[i] = given[i] + addition
            rest = rest - addition
    return np.array(given)


def noise(key, shape, spread, reach, cuts=(), held_as=jnp.bfloat16):
    array = spread * jax.random.normal(key, shape, jnp.float32)
    if cuts:
        array = array * block_levels(key, shape, cuts, -0.22, 0.18)
    return jnp.clip(array, -reach, reach).astype(held_as)


def noise_with(rng, dims, spread, reach, shards, heavy, kind=jnp.bfloat16):
    drawn = spread * jax.random.normal(rng, dims, jnp.float32)
    if shards:
        drawn = drawn * block_levels(rng, dims, shards, -0.22, 0.18)
    return jnp.clip(with_spikes(drawn, jax.random.fold_in(rng, 3), *heavy), -reach, reach).astype(kind)


def setup_inputs(seed: int = 0) -> dict:
    streams_of = jax.random.split(jax.random.key(seed), 6)
    grad_out = noise(streams_of[0], (N_SECTION, TOKENS, D), 1.0, 6.0, ((0, 3), (1, 256)))
    routes_keys = jax.random.split(jax.random.fold_in(streams_of[1], 1), N_SECTION * TOKENS // TOK_DEV)
    routes_turns = jax.random.permutation(jax.random.fold_in(streams_of[1], 3), N_SECTION * TOKENS // TOK_DEV)
    routes = jax.vmap(lambda own, number: assign_block(jax.random.fold_in(streams_of[1], 2), own, number, TOK_DEV, EXPERTS, TOPK, CAP, 2))(routes_keys, routes_turns).reshape((N_SECTION, TOKENS, TOPK))
    gates = jnp.clip(0.2 + 0.8 * jax.random.uniform(streams_of[2], (N_SECTION, TOKENS, TOPK), jnp.float32) ** block_levels(streams_of[2], (N_SECTION, TOKENS, TOPK), ((0, 3), (1, 256)), -0.2, 0.2), 0.2, 1.0)
    hidden = noise_with(streams_of[3], (N_SECTION, N_DP, EXPERTS, SLOTS, H), 0.015625, 0.09375, ((0, 3), (1, 16), (2, 16)), (1, 4, 16, 2.0))
    w_down = noise(streams_of[4], (N_SECTION, EXPERTS, H, D), H ** -0.5, 0.15625, ((0, 3), (1, 16)))
    return {"grad_out": grad_out, "routes": routes, "gates": gates, "hidden": hidden, "w_down": w_down}


def dispatch_block(rows, ids, weights, count, width):
    flat_ids = ids.reshape(-1).astype(jnp.int32)
    onehot = (flat_ids[:, None] == jnp.arange(count, dtype=jnp.int32)[None, :]).astype(jnp.int32)
    position = jnp.sum((jnp.cumsum(onehot, axis=0) - 1) * onehot, axis=1).astype(jnp.int32)
    target = flat_ids * width + position
    scaled = (weights[:, :, None].astype(jnp.float32) * rows[:, None, :].astype(jnp.float32)).astype(jnp.bfloat16)
    scaled = scaled.reshape(-1, rows.shape[1])
    buffer = jnp.zeros((count * width, rows.shape[1]), jnp.bfloat16).at[target].set(scaled)
    return buffer.reshape(count, width, rows.shape[1])


def reference(grad_out, routes, gates, hidden, w_down):
    incoming = jnp.roll(grad_out, -1, axis=0)
    hidden_grads = []
    weight_grads = []
    for section_id in range(N_SECTION):
        rows = incoming[section_id].reshape(N_DP * N_EXPERT, TOK_DEV, D)
        ids = routes[section_id].reshape(N_DP * N_EXPERT, TOK_DEV, TOPK)
        weights = gates[section_id].reshape(N_DP * N_EXPERT, TOK_DEV, TOPK)
        sent = jax.vmap(lambda r, i, w: dispatch_block(r, i, w, EXPERTS, CAP))(rows, ids, weights)
        sent = sent.reshape(N_DP, N_EXPERT, EXPERTS, CAP, D)
        scaled = sent.transpose(2, 0, 1, 3, 4).reshape(EXPERTS, N_DP, SLOTS, D)
        saved = hidden[section_id].transpose(1, 0, 2, 3)

        def one_expert(inputs):
            cot, hid, weight = inputs
            dh = jnp.einsum('dsk,hk->dsh', cot.astype(jnp.float32), weight.astype(jnp.float32)).astype(jnp.bfloat16)

            def add_group(total, pair):
                term = jnp.dot(pair[1].T, pair[0], preferred_element_type=jnp.float32).astype(jnp.bfloat16)
                term = lax.optimization_barrier(term)
                return total + term.astype(jnp.float32), None

            total, _ = lax.scan(add_group, jnp.zeros((H, D), jnp.float32), (cot, hid))
            return dh, total

        dh_all, dw_all = lax.map(one_expert, (scaled, saved, w_down[section_id]))
        hidden_grads.append(dh_all.transpose(1, 0, 2, 3))
        weight_grads.append(dw_all)
    return jnp.stack(hidden_grads), jnp.stack(weight_grads)
```

```python
import functools

import jax
import jax.numpy as jnp
from jax import lax
from jax.experimental import pallas as pl
from jax.experimental.pallas import tpu as pltpu
from jax.sharding import PartitionSpec as P

MESH = pl.DeviceIdType.MESH
RING = 4
WIDE = 512
FOLD = 128
TILE = 16
BF16, F32 = jnp.bfloat16, jnp.float32


def iota(shape, dim):
    return lax.broadcasted_iota(jnp.int32, shape, dim)


def ones_where(mask):
    return jnp.where(mask, 1.0, 0.0)


def dot(left, right):
    return jnp.dot(left, right, preferred_element_type=F32)


def kernel(
    counts, grad_ref, routes_ref, gates_ref, hidden_ref, w_ref, gh_ref, dw_ref,
    inc, send, recv, pick_a, pick_b, place_a, place_b, scaled, hid, hid_t, wv, part, xr1, xr2, col, zr1, zr2, ghv, dwv,
    in_sem, shift_s, shift_r, all_s, all_r, x_s, x_r, z_s, z_r, dw_sem, gh_sem,
):
    n_sec, n_dp, n_exp = counts
    tok, width = grad_ref.shape[1:]
    slots, units = hid.shape
    cap = slots // n_exp
    own_rows = units // n_dp
    block = 2 * own_rows
    chunks = width // WIDE
    padded = hid_t.shape[1]
    rows = TILE * n_exp
    half_x = RING // 2 * block
    half_z = (block // TILE + 1) // 2 * TILE

    sec, dp, ex = lax.axis_index("section"), lax.axis_index("dp"), lax.axis_index("expert")
    xi, zi = lax.rem(dp, RING), lax.div(dp, RING)
    x_up, x_down = lax.rem(xi + 1, RING), lax.rem(xi + RING - 1, RING)
    z_up, z_down = lax.rem(zi + 1, RING), lax.rem(zi + RING - 1, RING)
    x_far, z_far = lax.rem(xi + 2, RING), lax.rem(zi + 2, RING)
    to_x_up, to_x_down = {"dp": zi * RING + x_up}, {"dp": zi * RING + x_down}
    to_z_up, to_z_down = {"dp": z_up * RING + xi}, {"dp": z_down * RING + xi}
    before, after = {"section": lax.rem(sec + n_sec - 1, n_sec)}, {"section": lax.rem(sec + 1, n_sec)}

    barrier = pltpu.get_barrier_semaphore()

    def greet(to):
        pl.semaphore_signal(barrier, inc=1, device_id=to, device_id_type=MESH)

    for to in (before, after, to_x_up, to_x_down, to_z_up, to_z_down):
        greet(to)

    def greet_expert(i, carry):
        greet({"expert": lax.rem(ex + i, n_exp)})
        return carry

    lax.fori_loop(1, n_exp, greet_expert, 0)
    load_hidden = pltpu.make_async_copy(hidden_ref.at[0, 0, 0], hid, in_sem.at[0])
    load_w = pltpu.make_async_copy(w_ref.at[0, 0], wv, in_sem.at[1])
    load_hidden.start()
    pl.semaphore_wait(barrier, 6 + n_exp - 1)

    def remote(source, target, send_sem, recv_sem, to):
        return pltpu.make_async_remote_copy(
            src_ref=source, dst_ref=target, send_sem=send_sem, recv_sem=recv_sem, device_id=to, device_id_type=MESH
        )

    shifts = [
        remote(grad_ref.at[0, :, pl.ds(c * WIDE, WIDE)], inc.at[c], shift_s.at[c], shift_r.at[c], before)
        for c in range(chunks)
    ]
    for copy in shifts:
        copy.start()
    load_w.start()

    lane = iota((tok, FOLD), 1)
    named, gates = routes_ref[0].astype(F32), gates_ref[0]
    table = jnp.where(lane == 0, named[:, 0:1], jnp.where(lane == 1, named[:, 1:2], jnp.where(
        lane == 2, gates[:, 0:1], jnp.where(lane == 3, gates[:, 1:2], 0.0))))
    table = table.T
    expert = lax.shift_right_logical(iota((rows, tok), 0), 4).astype(F32)
    place = jnp.bitwise_and(iota((rows, tok), 0), TILE - 1)
    first, second = table[0:1] == expert, table[1:2] == expert
    active = ones_where(first | second)
    gate = jnp.where(first, table[2:3], jnp.where(second, table[3:4], 0.0))
    earlier = ones_where(iota((tok, tok), 0) < iota((tok, tok), 1)).astype(BF16)
    slot = dot(active.astype(BF16), earlier)
    hit_a = jnp.where(slot == place.astype(F32), active, 0.0)
    hit_b = jnp.where(slot == (TILE + jnp.bitwise_and(place, 3)).astype(F32), active, 0.0)
    gate_a = jnp.sum(hit_a * gate, axis=1, keepdims=True)
    gate_b = jnp.sum(hit_b * gate, axis=1, keepdims=True)
    pick_a[...] = hit_a.astype(BF16)
    quarter = lax.shift_right_logical(place, 2)
    for q in range(4):
        pick_b[:, q * tok:(q + 1) * tok] = jnp.where(quarter == q, hit_b, 0.0).astype(BF16)

    def exchange(c, start):
        mine = pl.ds(pl.multiple_of(ex * TILE, TILE), TILE)

        def one(i, carry):
            to = lax.rem(ex + i, n_exp)
            theirs = pl.ds(pl.multiple_of(to * TILE, TILE), TILE)
            remote(send.at[c, theirs], recv.at[c, mine], all_s.at[c], all_r.at[c], {"expert": to}).start()
            return carry

        lax.fori_loop(1, n_exp, one, 0)
        pltpu.make_async_copy(send.at[c, mine], recv.at[c, mine], all_r.at[c]).start()

    def dispatch(c):
        shifts[c].wait_recv()
        x = inc[c]
        send[c, :, 0:WIDE] = (dot(pick_a[...], x) * gate_a).astype(BF16)
        stacked = jnp.concatenate([x[:, q * FOLD:(q + 1) * FOLD] for q in range(4)], axis=0)
        send[c, :, WIDE:WIDE + FOLD] = (dot(pick_b[...], stacked) * gate_b).astype(BF16)
        exchange(c, True)

    dispatch(0)

    target, source = iota((padded, rows), 0), iota((padded, rows), 1)
    sender = lax.shift_right_logical(target * 3277, 16)
    index = target - sender * cap
    same = sender == lax.shift_right_logical(source, 4)
    at = jnp.bitwise_and(source, TILE - 1)
    place_a[...] = ones_where(same & (index == at)).astype(BF16)
    tail = same & (index == TILE + jnp.bitwise_and(at, 3))
    for q in range(4):
        place_b[q] = ones_where(tail & (lax.shift_right_logical(at, 2) == q)).astype(BF16)

    for c in range(1, chunks):
        dispatch(c)

    load_hidden.wait()
    for i in range(units // FOLD):
        piece = hid[:, i * FOLD:(i + 1) * FOLD].astype(F32)
        piece = jnp.concatenate([piece, jnp.zeros((padded - slots, FOLD), F32)], axis=0)
        hid_t[i * FOLD:(i + 1) * FOLD, :] = piece.T.astype(BF16)

    halves_x = (pl.ds(0, half_x), pl.ds(half_x, half_x))
    halves_z = (pl.ds(0, half_z), pl.ds(half_z, block - half_z))

    def z_rows(z, half):
        start = pl.multiple_of(z * block, TILE)
        return pl.ds(start, half_z) if half == 0 else pl.ds(start + half_z, block - half_z)

    def x_copies(c):
        a, b = halves_x

        def way(k, far, near, to):
            return (
                remote(part.at[c, x_far, far], xr1.at[c, k], x_s.at[c, k, 0], x_r.at[c, k, 0], to),
                remote(part.at[c, near[0], near[1]], xr2.at[c, k, near[1]], x_s.at[c, k, 1], x_r.at[c, k, 1], to),
                remote(part.at[c, near[0], far], xr2.at[c, k, far], x_s.at[c, k, 2], x_r.at[c, k, 2], to),
            )

        return way(0, a, (x_up, b), to_x_up), way(1, b, (x_down, a), to_x_down)

    def z_copies(c):
        def way(k, near, to):
            far_half = k
            far_rows, rest = halves_z[far_half], halves_z[1 - far_half]
            land = pl.ds(0, half_z if far_half == 0 else block - half_z)
            return (
                remote(col.at[c, z_rows(z_far, far_half)], zr1.at[c, k, land], z_s.at[c, k, 0], z_r.at[c, k, 0], to),
                remote(col.at[c, z_rows(near, 1 - far_half)], zr2.at[c, k, rest], z_s.at[c, k, 1], z_r.at[c, k, 1], to),
                remote(col.at[c, z_rows(near, far_half)], zr2.at[c, k, far_rows], z_s.at[c, k, 2], z_r.at[c, k, 2], to),
            )

        return way(0, z_up, to_z_up), way(1, z_down, to_z_down)

    xs, zs = [x_copies(c) for c in range(chunks)], [z_copies(c) for c in range(chunks)]

    def partial(c):
        pltpu.make_async_copy(recv.at[c], recv.at[c], all_r.at[c]).wait()
        head, tails = dot(place_a[...], recv[c, :, 0:WIDE]), recv[c, :, WIDE:WIDE + FOLD]
        for q in range(4):
            here = slice(c * WIDE + q * FOLD, c * WIDE + (q + 1) * FOLD)
            scaled[:, here] = (head[:, q * FOLD:(q + 1) * FOLD] + dot(place_b[q], tails)).astype(BF16)

        def group(z, carry):
            take = pl.ds(pl.multiple_of(z * RING * own_rows, TILE), RING * own_rows)
            out = dot(hid_t[take, :], scaled[:, c * WIDE:(c + 1) * WIDE])
            land = pl.ds(pl.multiple_of(z * block, TILE), block)
            for x in range(RING):
                mine = out[x * own_rows:(x + 1) * own_rows]
                both = jnp.concatenate([mine[:, :WIDE // 2], mine[:, WIDE // 2:]], axis=0)
                part[c, x, land, :] = both.astype(BF16)
            return carry

        lax.fori_loop(0, RING, group, 0)
        for step in (0, 1):
            for way in (0, 1):
                xs[c][way][step].start()

    def add(ref, at, other):
        ref[at] = (ref[at].astype(F32) + other.astype(F32)).astype(BF16)

    def relay_x(c):
        for way, near in ((0, x_up), (1, x_down)):
            xs[c][way][0].wait_recv()
            add(part, (c, near, halves_x[way]), xr1[c, way])
            xs[c][way][2].start()

    def column(c):
        for way in (0, 1):
            xs[c][way][1].wait_recv()
            xs[c][way][2].wait_recv()
        for z in range(RING):
            here = pl.ds(z * block, block)
            total = part[c, xi, here].astype(F32) + xr2[c, 0, here].astype(F32) + xr2[c, 1, here].astype(F32)
            col[c, here] = total.astype(BF16)
        for step in (0, 1):
            for way in (0, 1):
                zs[c][way][step].start()

    def relay_z(c):
        for way, near in ((0, z_up), (1, z_down)):
            size = half_z if way == 0 else block - half_z
            zs[c][way][0].wait_recv()
            add(col, (c, z_rows(near, way)), zr1[c, way, 0:size])
            zs[c][way][2].start()

    def store_dw(c):
        here = pl.ds(c * WIDE, WIDE)
        return pltpu.make_async_copy(dwv.at[:, here], dw_ref.at[0, 0, :, here], dw_sem.at[c])

    def finish(c):
        for way in (0, 1):
            zs[c][way][1].wait_recv()
            zs[c][way][2].wait_recv()
        here = pl.ds(pl.multiple_of(zi * block, TILE), block)
        total = col[c, here].astype(F32) + zr2[c, 0].astype(F32) + zr2[c, 1].astype(F32)
        dwv[:, c * WIDE:c * WIDE + WIDE // 2] = total[:own_rows]
        dwv[:, c * WIDE + WIDE // 2:(c + 1) * WIDE] = total[own_rows:]
        store_dw(c).start()

    store_gh = pltpu.make_async_copy(ghv, gh_ref.at[0, 0, 0], gh_sem)
    edges = list(range(0, units, 2 * FOLD)) + [units]
    pieces = list(zip(edges[:-1], edges[1:]))

    def hidden_grad(part_of, of):
        for low, high in pieces[part_of::of]:
            out = lax.dot_general(
                scaled[0:slots, :], wv[low:high, :], (((1,), (1,)), ((), ())), preferred_element_type=F32
            )
            ghv[:, low:high] = out.astype(BF16)

    for c in range(chunks + 3):
        if c < chunks:
            partial(c)
            relay_x(c)
            if c == chunks - 1:
                load_w.wait()
        if c >= chunks:
            hidden_grad(c - chunks, 3)
        if c >= 1 and c - 1 < chunks:
            column(c - 1)
        if c >= 2 and c - 2 < chunks:
            relay_z(c - 2)
        if c >= 3 and c - 3 < chunks:
            finish(c - 3)
    store_gh.start()

    for c in range(chunks):
        shifts[c].wait_send()
        sent = send.at[c, pl.ds(0, rows - TILE)]
        pltpu.make_async_copy(sent, sent, all_s.at[c]).wait()
        for ways in (xs[c], zs[c]):
            for way in ways:
                for copy in way:
                    copy.wait_send()
        store_dw(c).wait()
    store_gh.wait()


def shards(counts, grad_out, routes, gates, hidden, w_down):
    n_sec, n_dp, n_exp = counts
    tok, width = grad_out.shape[1:]
    slots, units = hidden.shape[3:]
    own_rows = units // n_dp
    block = 2 * own_rows
    chunks = width // WIDE
    padded = -(-slots // FOLD) * FOLD
    rows = TILE * n_exp
    half_x = RING // 2 * block
    half_z = (block // TILE + 1) // 2 * TILE
    half = WIDE // 2
    anywhere, vmem = pl.BlockSpec(memory_space=pl.ANY), pl.BlockSpec(memory_space=pltpu.VMEM)
    dma = pltpu.SemaphoreType.DMA
    return pl.pallas_call(
        functools.partial(kernel, counts),
        out_shape=(
            jax.ShapeDtypeStruct((1, 1, 1, slots, units), BF16),
            jax.ShapeDtypeStruct((1, 1, own_rows, width), F32),
        ),
        in_specs=[anywhere, vmem, vmem, anywhere, anywhere],
        out_specs=(anywhere, anywhere),
        scratch_shapes=[
            pltpu.VMEM((chunks, tok, WIDE), BF16),
            pltpu.VMEM((chunks, rows, WIDE + FOLD), BF16),
            pltpu.VMEM((chunks, rows, WIDE + FOLD), BF16),
            pltpu.VMEM((rows, tok), BF16),
            pltpu.VMEM((rows, 4 * tok), BF16),
            pltpu.VMEM((padded, rows), BF16),
            pltpu.VMEM((4, padded, rows), BF16),
            pltpu.VMEM((padded, width), BF16),
            pltpu.VMEM((slots, units), BF16),
            pltpu.VMEM((units, padded), BF16),
            pltpu.VMEM((units, width), BF16),
            pltpu.VMEM((chunks, RING, RING * block, half), BF16),
            pltpu.VMEM((chunks, 2, half_x, half), BF16),
            pltpu.VMEM((chunks, 2, RING * block, half), BF16),
            pltpu.VMEM((chunks, RING * block, half), BF16),
            pltpu.VMEM((chunks, 2, half_z, half), BF16),
            pltpu.VMEM((chunks, 2, block, half), BF16),
            pltpu.VMEM((slots, units), BF16),
            pltpu.VMEM((own_rows, width), F32),
            dma((2,)),
            dma((chunks,)),
            dma((chunks,)),
            dma((chunks,)),
            dma((chunks,)),
            dma((chunks, 2, 3)),
            dma((chunks, 2, 3)),
            dma((chunks, 2, 3)),
            dma((chunks, 2, 3)),
            dma((chunks,)),
            dma,
        ],
        compiler_params=pltpu.CompilerParams(
            collective_id=0, has_side_effects=True, vmem_limit_bytes=48 * 1024 * 1024
        ),
        name="relayed_backward",
    )(grad_out, routes, gates, hidden, w_down)


def solution(mesh):
    counts = tuple(mesh.shape[axis] for axis in ("section", "dp", "expert"))
    placed = (
        P("section", ("dp", "expert"), None),
        P("section", ("dp", "expert"), None),
        P("section", ("dp", "expert"), None),
        P("section", "dp", "expert", None, None),
        P("section", "expert", None, None),
    )
    return jax.shard_map(
        functools.partial(shards, counts),
        mesh=mesh,
        in_specs=placed,
        out_specs=(P("section", "dp", "expert", None, None), P("section", "expert", "dp", None)),
        check_vma=False,
    )
```

```python
import functools

import jax
import jax.numpy as jnp
from jax import lax
from jax.experimental import pallas as pl
from jax.experimental.pallas import tpu as pltpu
from jax.sharding import PartitionSpec as P

MESH = pl.DeviceIdType.MESH
RING = 4
WIDE = 512
FOLD = 128
TILE = 16
VMEM_BYTES = 60 * 1024 * 1024
BF16, F32 = jnp.bfloat16, jnp.float32


def iota(shape, dim):
    return lax.broadcasted_iota(jnp.int32, shape, dim)


def ones_where(mask):
    return jnp.where(mask, 1.0, 0.0)


def dot(left, right):
    return jnp.dot(left, right, preferred_element_type=F32)


def kernel(
    counts, grad_ref, routes_ref, gates_ref, hidden_ref, w_ref, gh_ref, dw_ref,
    inc, send, recv, pick_a, pick_b, place_a, place_b, scaled, hid, turned, far_hid, left, right, wv,
    out_x, in_x, own, col, zr1, zr2, ghv, dwv,
    in_sem, shift_s, shift_r, all_s, all_r, hid_s, hid_r, row_s, row_r, x_s, x_r, z_s, z_r, dw_sem, gh_sem,
):
    n_sec, n_dp, n_exp = counts
    tok, width = grad_ref.shape[1:]
    slots, units = hid.shape
    cap = slots // n_exp
    own_rows = units // n_dp
    group = RING * own_rows
    chunks = width // WIDE
    half = WIDE // 2
    padded = turned.shape[1]
    rows = TILE * n_exp

    sec, dp, ex = lax.axis_index("section"), lax.axis_index("dp"), lax.axis_index("expert")
    xi, zi = lax.rem(dp, RING), lax.div(dp, RING)
    odd = lax.rem(xi, 2)
    beside = (xi + 1 - 2 * odd, lax.rem(xi + RING - 1 + 2 * odd, RING))
    x_far, z_far = lax.rem(xi + 2, RING), lax.rem(zi + 2, RING)
    z_up, z_down = lax.rem(zi + 1, RING), lax.rem(zi + RING - 1, RING)
    to_x = tuple({"dp": zi * RING + x} for x in beside)
    to_z = tuple({"dp": z * RING + xi} for z in (z_up, z_down))
    before, after = {"section": lax.rem(sec + n_sec - 1, n_sec)}, {"section": lax.rem(sec + 1, n_sec)}

    barrier = pltpu.get_barrier_semaphore()

    def greet(to):
        pl.semaphore_signal(barrier, inc=1, device_id=to, device_id_type=MESH)

    for to in (before, after, *to_x, *to_z):
        greet(to)

    def greet_expert(i, carry):
        greet({"expert": lax.rem(ex + i, n_exp)})
        return carry

    lax.fori_loop(1, n_exp, greet_expert, 0)
    load_hidden = pltpu.make_async_copy(hidden_ref.at[0, 0, 0], hid, in_sem.at[0])
    load_w = pltpu.make_async_copy(w_ref.at[0, 0], wv, in_sem.at[1])
    load_hidden.start()
    pl.semaphore_wait(barrier, 6 + n_exp - 1)

    def remote(source, target, send_sem, recv_sem, to):
        return pltpu.make_async_remote_copy(
            src_ref=source, dst_ref=target, send_sem=send_sem, recv_sem=recv_sem, device_id=to, device_id_type=MESH
        )

    shifts = [
        remote(grad_ref.at[0, :, pl.ds(c * WIDE, WIDE)], inc.at[c], shift_s.at[c], shift_r.at[c], before)
        for c in range(chunks)
    ]
    for copy in shifts:
        copy.start()

    named, gates = routes_ref[0].astype(F32), gates_ref[0]
    expert = lax.shift_right_logical(iota((rows, tok), 0), 4).astype(F32)
    place = jnp.bitwise_and(iota((rows, tok), 0), TILE - 1)
    first, second = named[0:1] == expert, named[1:2] == expert
    active = ones_where(first | second)
    gate = jnp.where(first, gates[0:1], jnp.where(second, gates[1:2], 0.0))
    earlier = ones_where(iota((tok, tok), 0) < iota((tok, tok), 1)).astype(BF16)
    slot = dot(active.astype(BF16), earlier)
    hit_a = jnp.where(slot == place.astype(F32), active, 0.0)
    hit_b = jnp.where(slot == (TILE + jnp.bitwise_and(place, 3)).astype(F32), active, 0.0)
    gate_a = jnp.sum(hit_a * gate, axis=1, keepdims=True)
    gate_b = jnp.sum(hit_b * gate, axis=1, keepdims=True)
    pick_a[...] = hit_a.astype(BF16)
    quarter = lax.shift_right_logical(place, 2)
    for q in range(4):
        pick_b[:, q * tok:(q + 1) * tok] = jnp.where(quarter == q, hit_b, 0.0).astype(BF16)

    def exchange(c):
        mine = pl.ds(pl.multiple_of(ex * TILE, TILE), TILE)

        def one(i, carry):
            to = lax.rem(ex + i, n_exp)
            theirs = pl.ds(pl.multiple_of(to * TILE, TILE), TILE)
            remote(send.at[c, theirs], recv.at[c, mine], all_s.at[c], all_r.at[c], {"expert": to}).start()
            return carry

        lax.fori_loop(1, n_exp, one, 0)
        pltpu.make_async_copy(send.at[c, mine], recv.at[c, mine], all_r.at[c]).start()

    def dispatch(c):
        shifts[c].wait_recv()
        x = inc[c]
        send[c, :, 0:WIDE] = (dot(pick_a[...], x) * gate_a).astype(BF16)
        stacked = jnp.concatenate([x[:, q * FOLD:(q + 1) * FOLD] for q in range(4)], axis=0)
        send[c, :, WIDE:WIDE + FOLD] = (dot(pick_b[...], stacked) * gate_b).astype(BF16)
        exchange(c)

    top, low = pl.ds(0, group), pl.ds(group, group)
    mine_k, other_k = pl.ds(0, padded), pl.ds(padded, padded)
    give_hidden = [
        (
            remote(far_hid, left.at[h, top, other_k], hid_s.at[h, 0], hid_r.at[h, 0], to_x[h]),
            remote(left.at[1 - h, top, mine_k], left.at[h, low, other_k], hid_s.at[h, 1], hid_r.at[h, 1], to_x[h]),
        )
        for h in (0, 1)
    ]

    def turn_hidden():
        load_hidden.wait()
        for i in range(units // FOLD):
            piece = hid[:, i * FOLD:(i + 1) * FOLD].astype(F32)
            piece = jnp.concatenate([piece, jnp.zeros((padded - slots, FOLD), F32)], axis=0)
            turned[i * FOLD:(i + 1) * FOLD, :] = piece.T

        def of_owner(x):
            starts = [pl.multiple_of((z * RING + x) * own_rows, 8) for z in range(RING)]
            return jnp.concatenate([turned[pl.ds(start, own_rows), :] for start in starts], axis=0).astype(BF16)

        far_hid[...] = of_owner(x_far)
        for h in (0, 1):
            give_hidden[h][0].start()
        for h in (0, 1):
            left[1 - h, 0:group, 0:padded] = of_owner(beside[h])
            give_hidden[h][1].start()
        mine = of_owner(xi)
        for h in (0, 1):
            left[h, group:2 * group, 0:padded] = mine

    give_rows = [
        [
            remote(right.at[c, h, pl.ds(0, slots)], right.at[c, h, pl.ds(padded, slots)],
                   row_s.at[c, h], row_r.at[c, h], to_x[h])
            for h in (0, 1)
        ]
        for c in range(chunks)
    ]
    give_sums = [
        [remote(out_x.at[c, h], in_x.at[c, h], x_s.at[c, h], x_r.at[c, h], to_x[1 - h]) for h in (0, 1)]
        for c in range(chunks)
    ]

    def z_copies(c):
        return [
            (
                remote(col.at[c, k, z_far], zr1.at[c, k], z_s.at[c, k, 0], z_r.at[c, k, 0], to_z[k]),
                remote(col.at[c, 1 - k, near], zr2.at[c, k, 1 - k], z_s.at[c, k, 1], z_r.at[c, k, 1], to_z[k]),
                remote(col.at[c, k, near], zr2.at[c, k, k], z_s.at[c, k, 2], z_r.at[c, k, 2], to_z[k]),
            )
            for k, near in ((0, z_up), (1, z_down))
        ]

    zs = [z_copies(c) for c in range(chunks)]

    def collect(c):
        pltpu.make_async_copy(recv.at[c], recv.at[c], all_r.at[c]).wait()
        head, tails = dot(place_a[...], recv[c, :, 0:WIDE]), recv[c, :, WIDE:WIDE + FOLD]
        for q in range(4):
            block = (head[:, q * FOLD:(q + 1) * FOLD] + dot(place_b[q], tails)).astype(BF16)
            h, at = q // 2, q % 2 * FOLD
            right[c, h, 0:padded, at:at + FOLD] = block
            scaled[:, c * WIDE + q * FOLD:c * WIDE + (q + 1) * FOLD] = block[0:slots]
        for h in (0, 1):
            give_rows[c][h].start()

    def multiply(c):
        for h in (0, 1):
            if c == 0:
                for copy in give_hidden[h]:
                    copy.wait_recv()
            give_rows[c][h].wait_recv()
            for which in (0, 1):
                out = dot(left[h, which * group:(which + 1) * group, :], right[c, h])
                for z in range(RING):
                    mine = out[z * own_rows:(z + 1) * own_rows]
                    both = jnp.concatenate([mine[:, :FOLD], mine[:, FOLD:]], axis=0)
                    if which == 0:
                        out_x[c, h, z] = both.astype(BF16)
                    else:
                        own[c, h, z] = both
                if which == 0:
                    give_sums[c][h].start()

    def column(c):
        for h in (0, 1):
            give_sums[c][h].wait_recv()
            col[c, h] = (own[c, h] + in_x[c, h].astype(F32)).astype(BF16)
        for step in (0, 1):
            for way in (0, 1):
                zs[c][way][step].start()

    def relay(c):
        for way, near in ((0, z_up), (1, z_down)):
            zs[c][way][0].wait_recv()
            col[c, way, near] = (col[c, way, near].astype(F32) + zr1[c, way].astype(F32)).astype(BF16)
            zs[c][way][2].start()

    def store_dw(c):
        here = pl.ds(c * WIDE, WIDE)
        return pltpu.make_async_copy(dwv.at[:, here], dw_ref.at[0, 0, :, here], dw_sem.at[c])

    def finish(c):
        for way in (0, 1):
            zs[c][way][1].wait_recv()
            zs[c][way][2].wait_recv()
        for h in (0, 1):
            total = col[c, h, zi].astype(F32) + zr2[c, 0, h].astype(F32) + zr2[c, 1, h].astype(F32)
            at = c * WIDE + h * half
            dwv[:, at:at + FOLD] = total[:own_rows]
            dwv[:, at + FOLD:at + half] = total[own_rows:]
        store_dw(c).start()

    store_gh = pltpu.make_async_copy(ghv, gh_ref.at[0, 0, 0], gh_sem)
    edges = list(range(0, units, half)) + [units]
    pieces = list(zip(edges[:-1], edges[1:]))

    def hidden_grad(part_of):
        for low_edge, high_edge in pieces[part_of::3]:
            out = lax.dot_general(
                scaled[...], wv[low_edge:high_edge, :], (((1,), (1,)), ((), ())), preferred_element_type=F32
            )
            ghv[:, low_edge:high_edge] = out.astype(BF16)

    dispatch(0)
    turn_hidden()
    load_w.start()

    target, source = iota((padded, rows), 0), iota((padded, rows), 1)
    sender = lax.shift_right_logical(target * 3277, 16)
    index = target - sender * cap
    same = sender == lax.shift_right_logical(source, 4)
    at = jnp.bitwise_and(source, TILE - 1)
    place_a[...] = ones_where(same & (index == at)).astype(BF16)
    tail = same & (index == TILE + jnp.bitwise_and(at, 3))
    for q in range(4):
        place_b[q] = ones_where(tail & (lax.shift_right_logical(at, 2) == q)).astype(BF16)
    for c in range(chunks):
        for h in (0, 1):
            right[c, h, padded + slots:2 * padded, :] = jnp.zeros((padded - slots, half), BF16)

    dispatch(1)
    for c in range(chunks):
        collect(c)
        if c == 0:
            for later in range(2, chunks):
                dispatch(later)
        if c >= 1:
            column(c - 1)
        if c == chunks - 1:
            load_w.wait()
            hidden_grad(0)
        multiply(c)
        if c >= 1:
            relay(c - 1)
        if c >= 2:
            finish(c - 2)
    hidden_grad(1)
    column(chunks - 1)
    hidden_grad(2)
    store_gh.start()
    finish(chunks - 2)
    relay(chunks - 1)
    finish(chunks - 1)

    for h in (0, 1):
        for copy in give_hidden[h]:
            copy.wait_send()
    for c in range(chunks):
        shifts[c].wait_send()
        sent = send.at[c, pl.ds(0, rows - TILE)]
        pltpu.make_async_copy(sent, sent, all_s.at[c]).wait()
        for copy in (*give_rows[c], *give_sums[c], *zs[c][0], *zs[c][1]):
            copy.wait_send()
        store_dw(c).wait()
    store_gh.wait()


def shards(counts, grad_out, routes, gates, hidden, w_down):
    n_sec, n_dp, n_exp = counts
    tok, width = grad_out.shape[1:]
    slots, units = hidden.shape[3:]
    own_rows = units // n_dp
    block = 2 * own_rows
    group = RING * own_rows
    chunks = width // WIDE
    padded = -(-slots // FOLD) * FOLD
    rows = TILE * n_exp
    half = WIDE // 2
    anywhere, vmem = pl.BlockSpec(memory_space=pl.ANY), pl.BlockSpec(memory_space=pltpu.VMEM)
    dma = pltpu.SemaphoreType.DMA
    return pl.pallas_call(
        functools.partial(kernel, counts),
        out_shape=(
            jax.ShapeDtypeStruct((1, 1, 1, slots, units), BF16),
            jax.ShapeDtypeStruct((1, 1, own_rows, width), F32),
        ),
        in_specs=[anywhere, vmem, vmem, anywhere, anywhere],
        out_specs=(anywhere, anywhere),
        scratch_shapes=[
            pltpu.VMEM((chunks, tok, WIDE), BF16),
            pltpu.VMEM((chunks, rows, WIDE + FOLD), BF16),
            pltpu.VMEM((chunks, rows, WIDE + FOLD), BF16),
            pltpu.VMEM((rows, tok), BF16),
            pltpu.VMEM((rows, 4 * tok), BF16),
            pltpu.VMEM((padded, rows), BF16),
            pltpu.VMEM((4, padded, rows), BF16),
            pltpu.VMEM((slots, width), BF16),
            pltpu.VMEM((slots, units), BF16),
            pltpu.VMEM((units, padded), F32),
            pltpu.VMEM((group, padded), BF16),
            pltpu.VMEM((2, 2 * group, 2 * padded), BF16),
            pltpu.VMEM((chunks, 2, 2 * padded, half), BF16),
            pltpu.VMEM((units, width), BF16),
            pltpu.VMEM((chunks, 2, RING, block, FOLD), BF16),
            pltpu.VMEM((chunks, 2, RING, block, FOLD), BF16),
            pltpu.VMEM((chunks, 2, RING, block, FOLD), F32),
            pltpu.VMEM((chunks, 2, RING, block, FOLD), BF16),
            pltpu.VMEM((chunks, 2, block, FOLD), BF16),
            pltpu.VMEM((chunks, 2, 2, block, FOLD), BF16),
            pltpu.VMEM((slots, units), BF16),
            pltpu.VMEM((own_rows, width), F32),
            dma((2,)),
            dma((chunks,)),
            dma((chunks,)),
            dma((chunks,)),
            dma((chunks,)),
            dma((2, 2)),
            dma((2, 2)),
            dma((chunks, 2)),
            dma((chunks, 2)),
            dma((chunks, 2)),
            dma((chunks, 2)),
            dma((chunks, 2, 3)),
            dma((chunks, 2, 3)),
            dma((chunks,)),
            dma,
        ],
        compiler_params=pltpu.CompilerParams(
            collective_id=0, has_side_effects=True, vmem_limit_bytes=VMEM_BYTES
        ),
        name="relayed_backward",
    )(grad_out, routes.transpose(0, 2, 1), gates.transpose(0, 2, 1), hidden, w_down)


def solution(mesh):
    counts = tuple(mesh.shape[axis] for axis in ("section", "dp", "expert"))
    placed = (
        P("section", ("dp", "expert"), None),
        P("section", ("dp", "expert"), None),
        P("section", ("dp", "expert"), None),
        P("section", "dp", "expert", None, None),
        P("section", "expert", None, None),
    )
    return jax.shard_map(
        functools.partial(shards, counts),
        mesh=mesh,
        in_specs=placed,
        out_specs=(P("section", "dp", "expert", None, None), P("section", "expert", "dp", None)),
        check_vma=False,
    )
```

```python
import functools

import jax
import jax.numpy as jnp
from jax import lax
from jax.experimental import pallas as pl
from jax.experimental.pallas import tpu as pltpu
from jax.sharding import PartitionSpec as P

MESH = pl.DeviceIdType.MESH
RING = 4
WIDE = 512
NARROW = 256
FOLD = 128
TILE = 16
LEAD = 2
FOLDINGS = ((4, 2), (2, 3))
KINDS = {WIDE: 0, NARROW: 1}
VMEM_BYTES = 48 * 1024 * 1024
BF16, F32 = jnp.bfloat16, jnp.float32


def iota(shape, dim):
    return lax.broadcasted_iota(jnp.int32, shape, dim)


def ones_where(mask):
    return jnp.where(mask, 1.0, 0.0)


def dot(left, right):
    return jnp.dot(left, right, preferred_element_type=F32)


def cut_up(width):
    wide = (width - 2 * NARROW) // WIDE
    widths = [NARROW] + [WIDE] * wide + [NARROW]
    return widths, [sum(widths[:c]) for c in range(len(widths))]


def block_rows(wide, own_rows):
    return 2 * own_rows if wide == WIDE else -(-own_rows // TILE) * TILE


def kernel(
    counts, grad_ref, routes_ref, gates_ref, hidden_ref, w_ref, gh_ref, dw_ref,
    inc, send, recv, pick_a, pick_bs, place_a, place_bs, scaled, hid, turned, far_hid, left, right, wv,
    out_x, in_x, own, col, zr1, zr2, ghv, dwv,
    in_sem, shift_s, shift_r, all_s, all_r, hid_s, hid_r, row_s, row_r, x_s, x_r, z_s, z_r, dw_sem, gh_sem,
):
    n_sec, n_dp, n_exp = counts
    tok, width = grad_ref.shape[1:]
    slots, units = hid.shape
    cap = slots // n_exp
    own_rows = units // n_dp
    group = RING * own_rows
    widths, starts_at = cut_up(width)
    chunks = len(widths)
    padded = turned.shape[1]
    rows = TILE * n_exp

    sec, dp, ex = lax.axis_index("section"), lax.axis_index("dp"), lax.axis_index("expert")
    xi, zi = lax.rem(dp, RING), lax.div(dp, RING)
    odd = lax.rem(xi, 2)
    beside = (xi + 1 - 2 * odd, lax.rem(xi + RING - 1 + 2 * odd, RING))
    x_far, z_far = lax.rem(xi + 2, RING), lax.rem(zi + 2, RING)
    z_up, z_down = lax.rem(zi + 1, RING), lax.rem(zi + RING - 1, RING)
    to_x = tuple({"dp": zi * RING + x} for x in beside)
    to_z = tuple({"dp": z * RING + xi} for z in (z_up, z_down))
    before, after = {"section": lax.rem(sec + n_sec - 1, n_sec)}, {"section": lax.rem(sec + 1, n_sec)}

    barrier = pltpu.get_barrier_semaphore()

    def greet(to):
        pl.semaphore_signal(barrier, inc=1, device_id=to, device_id_type=MESH)

    for to in (before, after, *to_x, *to_z):
        greet(to)

    def greet_expert(i, carry):
        greet({"expert": lax.rem(ex + i, n_exp)})
        return carry

    lax.fori_loop(1, n_exp, greet_expert, 0)
    load_hidden = pltpu.make_async_copy(hidden_ref.at[0, 0, 0], hid, in_sem.at[0])
    load_w = pltpu.make_async_copy(w_ref.at[0, 0], wv, in_sem.at[1])
    load_hidden.start()
    def remote(source, target, send_sem, recv_sem, to):
        return pltpu.make_async_remote_copy(
            src_ref=source, dst_ref=target, send_sem=send_sem, recv_sem=recv_sem, device_id=to, device_id_type=MESH
        )

    def columns(c):
        return pl.ds(starts_at[c], widths[c])

    def cells(c):
        return pl.ds(0, widths[c] + FOLD)

    shifts = [
        remote(grad_ref.at[0, :, columns(c)], inc.at[:, columns(c)], shift_s.at[c], shift_r.at[c], before)
        for c in range(chunks)
    ]
    named, gates = routes_ref[0].astype(F32), gates_ref[0]
    expert = lax.shift_right_logical(iota((rows, tok), 0), 4).astype(F32)
    place = jnp.bitwise_and(iota((rows, tok), 0), TILE - 1)
    first, second = named[0:1] == expert, named[1:2] == expert
    active = ones_where(first | second)
    gate = jnp.where(first, gates[0:1], jnp.where(second, gates[1:2], 0.0))
    earlier = ones_where(iota((tok, tok), 0) < iota((tok, tok), 1)).astype(BF16)
    slot = dot(active.astype(BF16), earlier)
    hit_a = jnp.where(slot == place.astype(F32), active, 0.0)
    gate_a = jnp.sum(hit_a * gate, axis=1, keepdims=True)
    pick_a[...] = hit_a.astype(BF16)
    gate_bs = []
    for pick_b, (folds, depth_bits) in zip(pick_bs, FOLDINGS):
        late = TILE + jnp.bitwise_and(place, TILE // folds - 1)
        hit_b = jnp.where(slot == late.astype(F32), active, 0.0)
        gate_bs.append(jnp.sum(hit_b * gate, axis=1, keepdims=True))
        fold = lax.shift_right_logical(place, depth_bits)
        for q in range(folds):
            pick_b[:, q * tok:(q + 1) * tok] = jnp.where(fold == q, hit_b, 0.0).astype(BF16)

    def rows_of(e):
        return pl.ds(pl.multiple_of(e * TILE, TILE), TILE)

    def exchange(c):
        def one(i, carry):
            to = lax.rem(ex + lax.rem(i, 2) * ((i + 1) // 2) + (1 - lax.rem(i, 2)) * (n_exp - i // 2), n_exp)

            remote(
                send.at[c, rows_of(to), cells(c)], recv.at[c, rows_of(ex), cells(c)],
                all_s.at[c], all_r.at[c], {"expert": to},
            ).start()
            return carry

        lax.fori_loop(1, n_exp, one, 0)
        pltpu.make_async_copy(
            send.at[c, rows_of(ex), cells(c)], recv.at[c, rows_of(ex), cells(c)], all_r.at[c]
        ).start()

    def dispatch(c):
        shifts[c].wait_recv()
        if c + 1 < chunks:
            shifts[c + 1].start()
        wide, kind = widths[c], KINDS[widths[c]]
        x = inc[:, columns(c)]
        send[c, :, 0:wide] = (dot(pick_a[...], x) * gate_a).astype(BF16)
        stacked = jnp.concatenate([x[:, q * FOLD:(q + 1) * FOLD] for q in range(wide // FOLD)], axis=0)
        send[c, :, wide:wide + FOLD] = (dot(pick_bs[kind][...], stacked) * gate_bs[kind]).astype(BF16)

    top, low = pl.ds(0, group), pl.ds(group, group)
    mine_k, other_k = pl.ds(0, padded), pl.ds(padded, padded)
    give_hidden = [
        (
            remote(far_hid, left.at[h, top, other_k], hid_s.at[h, 0], hid_r.at[h, 0], to_x[h]),
            remote(left.at[1 - h, top, mine_k], left.at[h, low, other_k], hid_s.at[h, 1], hid_r.at[h, 1], to_x[h]),
        )
        for h in (0, 1)
    ]

    def turn_hidden():
        load_hidden.wait()
        for i in range(units // FOLD):
            piece = hid[:, i * FOLD:(i + 1) * FOLD].astype(F32)
            piece = jnp.concatenate([piece, jnp.zeros((padded - slots, FOLD), F32)], axis=0)
            turned[i * FOLD:(i + 1) * FOLD, :] = piece.T

        def of_owner(x):
            starts = [pl.multiple_of((z * RING + x) * own_rows, 8) for z in range(RING)]
            return jnp.concatenate([turned[pl.ds(start, own_rows), :] for start in starts], axis=0).astype(BF16)

        far_hid[...] = of_owner(x_far)
        for h in (0, 1):
            give_hidden[h][0].start()
        for h in (0, 1):
            left[1 - h, 0:group, 0:padded] = of_owner(beside[h])
            give_hidden[h][1].start()
        mine = of_owner(xi)
        for h in (0, 1):
            left[h, group:2 * group, 0:padded] = mine

    give_rows = [
        [
            remote(right[c].at[h, pl.ds(0, slots)], right[c].at[h, pl.ds(padded, slots)],
                   row_s.at[c, h], row_r.at[c, h], to_x[h])
            for h in (0, 1)
        ]
        for c in range(chunks)
    ]
    give_sums = [
        [remote(out_x[c].at[h], in_x[c].at[h], x_s.at[c, h], x_r.at[c, h], to_x[1 - h]) for h in (0, 1)]
        for c in range(chunks)
    ]

    def z_copies(c):
        return [
            (
                remote(col[c].at[k, z_far], zr1[c].at[k], z_s.at[c, k, 0], z_r.at[c, k, 0], to_z[k]),
                remote(col[c].at[1 - k, near], zr2[c].at[k, 1 - k], z_s.at[c, k, 1], z_r.at[c, k, 1], to_z[k]),
                remote(col[c].at[k, near], zr2[c].at[k, k], z_s.at[c, k, 2], z_r.at[c, k, 2], to_z[k]),
            )
            for k, near in ((0, z_up), (1, z_down))
        ]

    zs = [z_copies(c) for c in range(chunks)]

    def collect(c):
        arrived = recv.at[c, :, cells(c)]
        pltpu.make_async_copy(arrived, arrived, all_r.at[c]).wait()
        wide, start, place_b = widths[c], starts_at[c], place_bs[KINDS[widths[c]]]
        head, tails = dot(place_a[...], recv[c, :, 0:wide]), recv[c, :, wide:wide + FOLD]
        folds = wide // FOLD
        for q in range(folds):
            block = (head[:, q * FOLD:(q + 1) * FOLD] + dot(place_b[q], tails)).astype(BF16)
            h, at = q // (folds // 2), q % (folds // 2) * FOLD
            right[c][h, 0:padded, at:at + FOLD] = block
            scaled[:, start + q * FOLD:start + (q + 1) * FOLD] = block[0:slots]
        for h in (0, 1):
            give_rows[c][h].start()

    def multiply(c):
        for h in (0, 1):
            if c == 0:
                for copy in give_hidden[h]:
                    copy.wait_recv()
            give_rows[c][h].wait_recv()
            for which in (0, 1):
                out = dot(left[h, which * group:(which + 1) * group, :], right[c][h])
                for z in range(RING):
                    mine = out[z * own_rows:(z + 1) * own_rows]
                    if widths[c] == WIDE:
                        mine = jnp.concatenate([mine[:, :FOLD], mine[:, FOLD:]], axis=0)
                    fill = block_rows(widths[c], own_rows) - mine.shape[0]
                    if fill:
                        mine = jnp.concatenate([mine, jnp.zeros((fill, FOLD), F32)], axis=0)
                    if which == 0:
                        out_x[c][h, z] = mine.astype(BF16)
                    else:
                        own[c][h, z] = mine
                if which == 0:
                    give_sums[c][h].start()

    def column(c):
        for h in (0, 1):
            give_sums[c][h].wait_recv()
            col[c][h] = (own[c][h] + in_x[c][h].astype(F32)).astype(BF16)
        for step in (0, 1):
            for way in (0, 1):
                zs[c][way][step].start()

    def relay(c):
        for way, near in ((0, z_up), (1, z_down)):
            zs[c][way][0].wait_recv()
            col[c][way, near] = (col[c][way, near].astype(F32) + zr1[c][way].astype(F32)).astype(BF16)
            zs[c][way][2].start()

    def store_dw(c):
        here = columns(c)
        return pltpu.make_async_copy(dwv.at[:, here], dw_ref.at[0, 0, :, here], dw_sem.at[c])

    def finish(c):
        for way in (0, 1):
            zs[c][way][1].wait_recv()
            zs[c][way][2].wait_recv()
        for h in (0, 1):
            total = col[c][h, zi].astype(F32) + zr2[c][0, h].astype(F32) + zr2[c][1, h].astype(F32)
            at = starts_at[c] + h * (widths[c] // 2)
            dwv[:, at:at + FOLD] = total[:own_rows]
            if widths[c] == WIDE:
                dwv[:, at + FOLD:at + 2 * FOLD] = total[own_rows:]
        store_dw(c).start()

    store_gh = pltpu.make_async_copy(ghv, gh_ref.at[0, 0, 0], gh_sem)
    edges = list(range(0, units, 2 * FOLD)) + [units]
    pieces = list(zip(edges[:-1], edges[1:]))

    def hidden_grad(part_of):
        for low_edge, high_edge in pieces[part_of::3]:
            out = lax.dot_general(
                scaled[...], wv[low_edge:high_edge, :], (((1,), (1,)), ((), ())), preferred_element_type=F32
            )
            ghv[:, low_edge:high_edge] = out.astype(BF16)

    pl.semaphore_wait(barrier, 6 + n_exp - 1)
    shifts[0].start()
    turn_hidden()
    dispatch(0)
    exchange(0)
    load_w.start()

    target, source = iota((padded, rows), 0), iota((padded, rows), 1)
    sender = lax.shift_right_logical(target * 3277, 16)
    index = target - sender * cap
    same = sender == lax.shift_right_logical(source, 4)
    at = jnp.bitwise_and(source, TILE - 1)
    place_a[...] = ones_where(same & (index == at)).astype(BF16)
    for place_b, (folds, depth_bits) in zip(place_bs, FOLDINGS):
        late = same & (index == TILE + jnp.bitwise_and(at, TILE // folds - 1))
        for q in range(folds):
            place_b[q] = ones_where(late & (lax.shift_right_logical(at, depth_bits) == q)).astype(BF16)
    for c in range(chunks):
        for h in (0, 1):
            right[c][h, padded + slots:2 * padded, :] = jnp.zeros((padded - slots, widths[c] // 2), BF16)

    for c in range(1, LEAD):
        dispatch(c)
        exchange(c)
    for c in range(chunks):
        collect(c)
        if c + LEAD < chunks:
            dispatch(c + LEAD)
            exchange(c + LEAD)
        if c >= 2:
            relay(c - 2)
        if c == chunks - 1:
            load_w.wait()
            hidden_grad(0)
        if c >= 1:
            column(c - 1)
        multiply(c)
        if c >= 3:
            finish(c - 3)
    relay(chunks - 2)
    hidden_grad(1)
    column(chunks - 1)
    hidden_grad(2)
    store_gh.start()
    finish(chunks - 3)
    relay(chunks - 1)
    finish(chunks - 2)
    finish(chunks - 1)

    for h in (0, 1):
        for copy in give_hidden[h]:
            copy.wait_send()
    for c in range(chunks):
        shifts[c].wait_send()
        sent = send.at[c, pl.ds(0, rows - TILE), cells(c)]
        pltpu.make_async_copy(sent, sent, all_s.at[c]).wait()
        for copy in (*give_rows[c], *give_sums[c], *zs[c][0], *zs[c][1]):
            copy.wait_send()
        store_dw(c).wait()
    store_gh.wait()


def shards(counts, grad_out, routes, gates, hidden, w_down):
    n_sec, n_dp, n_exp = counts
    tok, width = grad_out.shape[1:]
    slots, units = hidden.shape[3:]
    own_rows = units // n_dp
    group = RING * own_rows
    widths, _ = cut_up(width)
    chunks = len(widths)
    padded = -(-slots // FOLD) * FOLD
    rows = TILE * n_exp
    blocks = [block_rows(wide, own_rows) for wide in widths]
    hbm, anywhere = pl.BlockSpec(memory_space=pltpu.HBM), pl.BlockSpec(memory_space=pl.ANY)
    vmem = pl.BlockSpec(memory_space=pltpu.VMEM)
    dma = pltpu.SemaphoreType.DMA
    return pl.pallas_call(
        functools.partial(kernel, counts),
        out_shape=(
            jax.ShapeDtypeStruct((1, 1, 1, slots, units), BF16),
            jax.ShapeDtypeStruct((1, 1, own_rows, width), F32),
        ),
        in_specs=[hbm, vmem, vmem, hbm, hbm],
        out_specs=(anywhere, anywhere),
        scratch_shapes=[
            pltpu.VMEM((tok, width), BF16),
            pltpu.VMEM((chunks, rows, WIDE + FOLD), BF16),
            pltpu.VMEM((chunks, rows, WIDE + FOLD), BF16),
            pltpu.VMEM((rows, tok), BF16),
            tuple(pltpu.VMEM((rows, folds * tok), BF16) for folds, _ in FOLDINGS),
            pltpu.VMEM((padded, rows), BF16),
            tuple(pltpu.VMEM((folds, padded, rows), BF16) for folds, _ in FOLDINGS),
            pltpu.VMEM((slots, width), BF16),
            pltpu.VMEM((slots, units), BF16),
            pltpu.VMEM((units, padded), F32),
            pltpu.VMEM((group, padded), BF16),
            pltpu.VMEM((2, 2 * group, 2 * padded), BF16),
            tuple(pltpu.VMEM((2, 2 * padded, wide // 2), BF16) for wide in widths),
            pltpu.VMEM((units, width), BF16),
            tuple(pltpu.VMEM((2, RING, block, FOLD), BF16) for block in blocks),
            tuple(pltpu.VMEM((2, RING, block, FOLD), BF16) for block in blocks),
            tuple(pltpu.VMEM((2, RING, block, FOLD), F32) for block in blocks),
            tuple(pltpu.VMEM((2, RING, block, FOLD), BF16) for block in blocks),
            tuple(pltpu.VMEM((2, block, FOLD), BF16) for block in blocks),
            tuple(pltpu.VMEM((2, 2, block, FOLD), BF16) for block in blocks),
            pltpu.VMEM((slots, units), BF16),
            pltpu.VMEM((own_rows, width), F32),
            dma((2,)),
            dma((chunks,)),
            dma((chunks,)),
            dma((chunks,)),
            dma((chunks,)),
            dma((2, 2)),
            dma((2, 2)),
            dma((chunks, 2)),
            dma((chunks, 2)),
            dma((chunks, 2)),
            dma((chunks, 2)),
            dma((chunks, 2, 3)),
            dma((chunks, 2, 3)),
            dma((chunks,)),
            dma,
        ],
        compiler_params=pltpu.CompilerParams(
            collective_id=0, has_side_effects=True, vmem_limit_bytes=VMEM_BYTES
        ),
        name="relayed_backward",
    )(grad_out, routes.transpose(0, 2, 1), gates.transpose(0, 2, 1), hidden, w_down)


def solution(mesh):
    counts = tuple(mesh.shape[axis] for axis in ("section", "dp", "expert"))
    placed = (
        P("section", ("dp", "expert"), None),
        P("section", ("dp", "expert"), None),
        P("section", ("dp", "expert"), None),
        P("section", "dp", "expert", None, None),
        P("section", "expert", None, None),
    )
    return jax.shard_map(
        functools.partial(shards, counts),
        mesh=mesh,
        in_specs=placed,
        out_specs=(P("section", "dp", "expert", None, None), P("section", "expert", "dp", None)),
        check_vma=False,
    )
```

```python
import functools

import jax
import jax.numpy as jnp
from jax import lax
from jax.experimental import pallas as pl
from jax.experimental.pallas import tpu as pltpu
from jax.sharding import PartitionSpec as P

MESH = pl.DeviceIdType.MESH
RING = 4
WIDE = 512
NARROW = 256
FOLD = 128
TILE = 16
LEAD = 2
FOLDINGS = ((4, 2), (2, 3))
KINDS = {WIDE: 0, NARROW: 1}
VMEM_BYTES = 48 * 1024 * 1024
BF16, F32 = jnp.bfloat16, jnp.float32


def iota(shape, dim):
    return lax.broadcasted_iota(jnp.int32, shape, dim)


def ones_where(mask):
    return jnp.where(mask, 1.0, 0.0)


def dot(left, right):
    return jnp.dot(left, right, preferred_element_type=F32)


def cut_up(width):
    wide = (width - 2 * NARROW) // WIDE
    widths = [NARROW] + [WIDE] * wide + [NARROW]
    return widths, [sum(widths[:c]) for c in range(len(widths))]


def block_rows(wide, own_rows):
    return 2 * own_rows if wide == WIDE else -(-own_rows // TILE) * TILE


def kernel(
    counts, grad_ref, routes_ref, gates_ref, hidden_ref, w_ref, gh_ref, dw_ref,
    inc, send, recv, pick_a, pick_bs, place_a, place_bs, scaled, hid, turned, far_hid, left, right, wv,
    out_x, in_x, own, col, zr1, zr2, ghv, dwv,
    in_sem, shift_s, shift_r, all_s, all_r, hid_s, hid_r, row_s, row_r, x_s, x_r, z_s, z_r, dw_sem, gh_sem,
):
    n_sec, n_dp, n_exp = counts
    tok, width = grad_ref.shape[1:]
    slots, units = hid.shape
    cap = slots // n_exp
    own_rows = units // n_dp
    group = RING * own_rows
    widths, starts_at = cut_up(width)
    chunks = len(widths)
    padded = turned.shape[1]
    rows = TILE * n_exp

    sec, dp, ex = lax.axis_index("section"), lax.axis_index("dp"), lax.axis_index("expert")
    xi, zi = lax.rem(dp, RING), lax.div(dp, RING)
    odd = lax.rem(xi, 2)
    beside = (xi + 1 - 2 * odd, lax.rem(xi + RING - 1 + 2 * odd, RING))
    x_far, z_far = lax.rem(xi + 2, RING), lax.rem(zi + 2, RING)
    z_up, z_down = lax.rem(zi + 1, RING), lax.rem(zi + RING - 1, RING)
    to_x = tuple({"dp": zi * RING + x} for x in beside)
    to_z = tuple({"dp": z * RING + xi} for z in (z_up, z_down))
    before, after = {"section": lax.rem(sec + n_sec - 1, n_sec)}, {"section": lax.rem(sec + 1, n_sec)}

    barrier = pltpu.get_barrier_semaphore()

    def greet(to):
        pl.semaphore_signal(barrier, inc=1, device_id=to, device_id_type=MESH)

    for to in (before, after, *to_x, *to_z):
        greet(to)

    def greet_expert(i, carry):
        greet({"expert": lax.rem(ex + i, n_exp)})
        return carry

    lax.fori_loop(1, n_exp, greet_expert, 0)
    load_hidden = pltpu.make_async_copy(hidden_ref.at[0, 0, 0], hid, in_sem.at[0])
    load_w = pltpu.make_async_copy(w_ref.at[0, 0], wv, in_sem.at[1])
    load_hidden.start()
    def remote(source, target, send_sem, recv_sem, to):
        return pltpu.make_async_remote_copy(
            src_ref=source, dst_ref=target, send_sem=send_sem, recv_sem=recv_sem, device_id=to, device_id_type=MESH
        )

    def columns(c):
        return pl.ds(starts_at[c], widths[c])

    def cells(c):
        return pl.ds(0, widths[c] + FOLD)

    shifts = [
        remote(grad_ref.at[0, :, columns(c)], inc.at[:, columns(c)], shift_s.at[c], shift_r.at[c], before)
        for c in range(chunks)
    ]
    named, gates = routes_ref[0].astype(F32), gates_ref[0]
    expert = lax.shift_right_logical(iota((rows, tok), 0), 4).astype(F32)
    place = jnp.bitwise_and(iota((rows, tok), 0), TILE - 1)
    first, second = named[0:1] == expert, named[1:2] == expert
    active = ones_where(first | second)
    gate = jnp.where(first, gates[0:1], jnp.where(second, gates[1:2], 0.0))
    earlier = ones_where(iota((tok, tok), 0) < iota((tok, tok), 1)).astype(BF16)
    slot = dot(active.astype(BF16), earlier)
    hit_a = jnp.where(slot == place.astype(F32), active, 0.0)
    gate_a = jnp.sum(hit_a * gate, axis=1, keepdims=True)
    pick_a[...] = hit_a.astype(BF16)
    gate_bs = []
    for pick_b, (folds, depth_bits) in zip(pick_bs, FOLDINGS):
        late = TILE + jnp.bitwise_and(place, TILE // folds - 1)
        hit_b = jnp.where(slot == late.astype(F32), active, 0.0)
        gate_bs.append(jnp.sum(hit_b * gate, axis=1, keepdims=True))
        fold = lax.shift_right_logical(place, depth_bits)
        for q in range(folds):
            pick_b[:, q * tok:(q + 1) * tok] = jnp.where(fold == q, hit_b, 0.0).astype(BF16)

    def rows_of(e):
        return pl.ds(pl.multiple_of(e * TILE, TILE), TILE)

    def exchange(c):
        def one(i, carry):
            to = lax.rem(ex + lax.rem(i, 2) * ((i + 1) // 2) + (1 - lax.rem(i, 2)) * (n_exp - i // 2), n_exp)

            remote(
                send.at[c, rows_of(to), cells(c)], recv.at[c, rows_of(ex), cells(c)],
                all_s.at[c], all_r.at[c], {"expert": to},
            ).start()
            return carry

        lax.fori_loop(1, n_exp, one, 0)
        pltpu.make_async_copy(
            send.at[c, rows_of(ex), cells(c)], recv.at[c, rows_of(ex), cells(c)], all_r.at[c]
        ).start()

    def dispatch(c):
        shifts[c].wait_recv()
        if c + 1 < chunks:
            shifts[c + 1].start()
        wide, kind = widths[c], KINDS[widths[c]]
        x = inc[:, columns(c)]
        send[c, :, 0:wide] = (dot(pick_a[...], x) * gate_a).astype(BF16)
        stacked = jnp.concatenate([x[:, q * FOLD:(q + 1) * FOLD] for q in range(wide // FOLD)], axis=0)
        send[c, :, wide:wide + FOLD] = (dot(pick_bs[kind][...], stacked) * gate_bs[kind]).astype(BF16)

    top, low = pl.ds(0, group), pl.ds(group, group)
    mine_k, other_k = pl.ds(0, padded), pl.ds(padded, padded)
    give_hidden = [
        (
            remote(far_hid, left.at[h, top, other_k], hid_s.at[h, 0], hid_r.at[h, 0], to_x[h]),
            remote(left.at[1 - h, top, mine_k], left.at[h, low, other_k], hid_s.at[h, 1], hid_r.at[h, 1], to_x[h]),
        )
        for h in (0, 1)
    ]

    def turn_hidden():
        load_hidden.wait()
        for i in range(units // FOLD):
            piece = hid[:, i * FOLD:(i + 1) * FOLD].astype(F32)
            piece = jnp.concatenate([piece, jnp.zeros((padded - slots, FOLD), F32)], axis=0)
            turned[i * FOLD:(i + 1) * FOLD, :] = piece.T

        def of_owner(x):
            starts = [pl.multiple_of((z * RING + x) * own_rows, 8) for z in range(RING)]
            return jnp.concatenate([turned[pl.ds(start, own_rows), :] for start in starts], axis=0).astype(BF16)

        far_hid[...] = of_owner(x_far)
        for h in (0, 1):
            give_hidden[h][0].start()
        for h in (0, 1):
            left[1 - h, 0:group, 0:padded] = of_owner(beside[h])
            give_hidden[h][1].start()
        mine = of_owner(xi)
        for h in (0, 1):
            left[h, group:2 * group, 0:padded] = mine

    give_rows = [
        [
            remote(right[c].at[h, pl.ds(0, slots)], right[c].at[h, pl.ds(padded, slots)],
                   row_s.at[c, h], row_r.at[c, h], to_x[h])
            for h in (0, 1)
        ]
        for c in range(chunks)
    ]
    give_sums = [
        [remote(out_x[c].at[h], in_x[c].at[h], x_s.at[c, h], x_r.at[c, h], to_x[1 - h]) for h in (0, 1)]
        for c in range(chunks)
    ]

    def z_copies(c):
        return [
            (
                remote(col[c].at[k, z_far], zr1[c].at[k], z_s.at[c, k, 0], z_r.at[c, k, 0], to_z[k]),
                remote(col[c].at[1 - k, near], zr2[c].at[k, 1 - k], z_s.at[c, k, 1], z_r.at[c, k, 1], to_z[k]),
                remote(col[c].at[k, near], zr2[c].at[k, k], z_s.at[c, k, 2], z_r.at[c, k, 2], to_z[k]),
            )
            for k, near in ((0, z_up), (1, z_down))
        ]

    zs = [z_copies(c) for c in range(chunks)]

    def collect(c):
        arrived = recv.at[c, :, cells(c)]
        pltpu.make_async_copy(arrived, arrived, all_r.at[c]).wait()
        wide, start, place_b = widths[c], starts_at[c], place_bs[KINDS[widths[c]]]
        head, tails = dot(place_a[...], recv[c, :, 0:wide]), recv[c, :, wide:wide + FOLD]
        folds = wide // FOLD
        for q in range(folds):
            block = (head[:, q * FOLD:(q + 1) * FOLD] + dot(place_b[q], tails)).astype(BF16)
            h, at = q // (folds // 2), q % (folds // 2) * FOLD
            right[c][h, 0:padded, at:at + FOLD] = block
            scaled[:, start + q * FOLD:start + (q + 1) * FOLD] = block[0:slots]
            if q % (folds // 2) == folds // 2 - 1:
                give_rows[c][h].start()

    def multiply(c):
        for h in (0, 1):
            if c == 0:
                for copy in give_hidden[h]:
                    copy.wait_recv()
            give_rows[c][h].wait_recv()
            for which in (0, 1):
                out = dot(left[h, which * group:(which + 1) * group, :], right[c][h])
                for z in range(RING):
                    mine = out[z * own_rows:(z + 1) * own_rows]
                    if widths[c] == WIDE:
                        mine = jnp.concatenate([mine[:, :FOLD], mine[:, FOLD:]], axis=0)
                    fill = block_rows(widths[c], own_rows) - mine.shape[0]
                    if fill:
                        mine = jnp.concatenate([mine, jnp.zeros((fill, FOLD), F32)], axis=0)
                    if which == 0:
                        out_x[c][h, z] = mine.astype(BF16)
                    else:
                        own[c][h, z] = mine
                if which == 0:
                    give_sums[c][h].start()

    def column(c):
        for h in (0, 1):
            give_sums[c][h].wait_recv()
            col[c][h] = (own[c][h] + in_x[c][h].astype(F32)).astype(BF16)
            zs[c][h][0].start()
            zs[c][1 - h][1].start()

    def relay(c):
        for way, near in ((0, z_up), (1, z_down)):
            zs[c][way][0].wait_recv()
            col[c][way, near] = (col[c][way, near].astype(F32) + zr1[c][way].astype(F32)).astype(BF16)
            zs[c][way][2].start()

    def store_dw(c):
        here = columns(c)
        return pltpu.make_async_copy(dwv.at[:, here], dw_ref.at[0, 0, :, here], dw_sem.at[c])

    def finish(c):
        for way in (0, 1):
            zs[c][way][1].wait_recv()
            zs[c][way][2].wait_recv()
        for h in (0, 1):
            total = col[c][h, zi].astype(F32) + zr2[c][0, h].astype(F32) + zr2[c][1, h].astype(F32)
            at = starts_at[c] + h * (widths[c] // 2)
            dwv[:, at:at + FOLD] = total[:own_rows]
            if widths[c] == WIDE:
                dwv[:, at + FOLD:at + 2 * FOLD] = total[own_rows:]
        store_dw(c).start()

    store_gh = pltpu.make_async_copy(ghv, gh_ref.at[0, 0, 0], gh_sem)
    edges = list(range(0, units, 2 * FOLD)) + [units]
    pieces = list(zip(edges[:-1], edges[1:]))

    def hidden_grad(part_of):
        for low_edge, high_edge in pieces[part_of::3]:
            out = lax.dot_general(
                scaled[...], wv[low_edge:high_edge, :], (((1,), (1,)), ((), ())), preferred_element_type=F32
            )
            ghv[:, low_edge:high_edge] = out.astype(BF16)

    pl.semaphore_wait(barrier, 6 + n_exp - 1)
    shifts[0].start()
    turn_hidden()
    dispatch(0)
    exchange(0)
    load_w.start()

    target, source = iota((padded, rows), 0), iota((padded, rows), 1)
    sender = lax.shift_right_logical(target * 3277, 16)
    index = target - sender * cap
    same = sender == lax.shift_right_logical(source, 4)
    at = jnp.bitwise_and(source, TILE - 1)
    place_a[...] = ones_where(same & (index == at)).astype(BF16)
    for place_b, (folds, depth_bits) in zip(place_bs, FOLDINGS):
        late = same & (index == TILE + jnp.bitwise_and(at, TILE // folds - 1))
        for q in range(folds):
            place_b[q] = ones_where(late & (lax.shift_right_logical(at, depth_bits) == q)).astype(BF16)
    for c in range(chunks):
        for h in (0, 1):
            right[c][h, padded + slots:2 * padded, :] = jnp.zeros((padded - slots, widths[c] // 2), BF16)

    for c in range(1, LEAD):
        dispatch(c)
        exchange(c)
    for c in range(chunks):
        collect(c)
        if c + LEAD < chunks:
            dispatch(c + LEAD)
            exchange(c + LEAD)
        if c >= 2:
            relay(c - 2)
        if c == chunks - 1:
            load_w.wait()
            hidden_grad(0)
        if c >= 1:
            column(c - 1)
        multiply(c)
        if c >= 3:
            finish(c - 3)
    relay(chunks - 2)
    hidden_grad(1)
    column(chunks - 1)
    hidden_grad(2)
    store_gh.start()
    finish(chunks - 3)
    relay(chunks - 1)
    finish(chunks - 2)
    finish(chunks - 1)

    for h in (0, 1):
        for copy in give_hidden[h]:
            copy.wait_send()
    for c in range(chunks):
        shifts[c].wait_send()
        sent = send.at[c, pl.ds(0, rows - TILE), cells(c)]
        pltpu.make_async_copy(sent, sent, all_s.at[c]).wait()
        for copy in (*give_rows[c], *give_sums[c], *zs[c][0], *zs[c][1]):
            copy.wait_send()
        store_dw(c).wait()
    store_gh.wait()


def shards(counts, grad_out, routes, gates, hidden, w_down):
    n_sec, n_dp, n_exp = counts
    tok, width = grad_out.shape[1:]
    slots, units = hidden.shape[3:]
    own_rows = units // n_dp
    group = RING * own_rows
    widths, _ = cut_up(width)
    chunks = len(widths)
    padded = -(-slots // FOLD) * FOLD
    rows = TILE * n_exp
    blocks = [block_rows(wide, own_rows) for wide in widths]
    hbm, anywhere = pl.BlockSpec(memory_space=pltpu.HBM), pl.BlockSpec(memory_space=pl.ANY)
    vmem = pl.BlockSpec(memory_space=pltpu.VMEM)
    dma = pltpu.SemaphoreType.DMA
    return pl.pallas_call(
        functools.partial(kernel, counts),
        out_shape=(
            jax.ShapeDtypeStruct((1, 1, 1, slots, units), BF16),
            jax.ShapeDtypeStruct((1, 1, own_rows, width), F32),
        ),
        in_specs=[hbm, vmem, vmem, hbm, hbm],
        out_specs=(anywhere, anywhere),
        scratch_shapes=[
            pltpu.VMEM((tok, width), BF16),
            pltpu.VMEM((chunks, rows, WIDE + FOLD), BF16),
            pltpu.VMEM((chunks, rows, WIDE + FOLD), BF16),
            pltpu.VMEM((rows, tok), BF16),
            tuple(pltpu.VMEM((rows, folds * tok), BF16) for folds, _ in FOLDINGS),
            pltpu.VMEM((padded, rows), BF16),
            tuple(pltpu.VMEM((folds, padded, rows), BF16) for folds, _ in FOLDINGS),
            pltpu.VMEM((slots, width), BF16),
            pltpu.VMEM((slots, units), BF16),
            pltpu.VMEM((units, padded), F32),
            pltpu.VMEM((group, padded), BF16),
            pltpu.VMEM((2, 2 * group, 2 * padded), BF16),
            tuple(pltpu.VMEM((2, 2 * padded, wide // 2), BF16) for wide in widths),
            pltpu.VMEM((units, width), BF16),
            tuple(pltpu.VMEM((2, RING, block, FOLD), BF16) for block in blocks),
            tuple(pltpu.VMEM((2, RING, block, FOLD), BF16) for block in blocks),
            tuple(pltpu.VMEM((2, RING, block, FOLD), F32) for block in blocks),
            tuple(pltpu.VMEM((2, RING, block, FOLD), BF16) for block in blocks),
            tuple(pltpu.VMEM((2, block, FOLD), BF16) for block in blocks),
            tuple(pltpu.VMEM((2, 2, block, FOLD), BF16) for block in blocks),
            pltpu.VMEM((slots, units), BF16),
            pltpu.VMEM((own_rows, width), F32),
            dma((2,)),
            dma((chunks,)),
            dma((chunks,)),
            dma((chunks,)),
            dma((chunks,)),
            dma((2, 2)),
            dma((2, 2)),
            dma((chunks, 2)),
            dma((chunks, 2)),
            dma((chunks, 2)),
            dma((chunks, 2)),
            dma((chunks, 2, 3)),
            dma((chunks, 2, 3)),
            dma((chunks,)),
            dma,
        ],
        compiler_params=pltpu.CompilerParams(
            collective_id=0, has_side_effects=True, vmem_limit_bytes=VMEM_BYTES
        ),
        name="relayed_backward",
    )(grad_out, routes.transpose(0, 2, 1), gates.transpose(0, 2, 1), hidden, w_down)


def solution(mesh):
    counts = tuple(mesh.shape[axis] for axis in ("section", "dp", "expert"))
    placed = (
        P("section", ("dp", "expert"), None),
        P("section", ("dp", "expert"), None),
        P("section", ("dp", "expert"), None),
        P("section", "dp", "expert", None, None),
        P("section", "expert", None, None),
    )
    return jax.shard_map(
        functools.partial(shards, counts),
        mesh=mesh,
        in_specs=placed,
        out_specs=(P("section", "dp", "expert", None, None), P("section", "expert", "dp", None)),
        check_vma=False,
    )
```
